32 devices in a mesh: grp: 2 (over y), ori: 4 (over z), ty: 2 (over x), tx: 2 (over core).
Axes of the slice: x: 2, y: 2, z: 4, core: 2. Of those that a mesh axis runs over, the one named last changes fastest.
Arguments:
- volume: float32 [32, 32, 64], P(('grp', 'ty'), 'tx'), parts along dimension 0, may hold values from -1000 to 1000
- templates: bfloat16 [128, 1728], P(('grp', 'ori')), parts along dimension 0, may hold values from -1 to 1, as said below
- prior_table: int32 [64], P('ori'), may hold values from 0 to 7
- moment_table: float32 [4, 64], P(None, 'ori'), may hold values from -6 to 6
Outputs:
- log_total: float32 [32, 32, 64], P(('grp', 'ty'), ('tx', 'ori')), parts along dimension 0
- moments: float32 [4, 32, 32, 64], P(None, ('grp', 'ty'), ('tx', 'ori')), parts along dimension 1
The draws below stay inside these ranges and needn't reach their ends.
There are 2 independent parts, one for each index of `grp`. The reference program is written for one: setup_inputs(seed, part) draws one part's arguments, and reference() takes and returns one part's arrays. A program takes and returns all parts, laid end to end along the dimension named above; an argument that names none is the same for every part. Nothing has to cross between parts.
Inputs may be any that keep to these rules, and one draw needn't show every extreme that they name: `templates`: each row has unit Euclidean norm up to rounding.
All inputs are finite; a program needn't handle non-finite values.
Results may differ from the reference program's by a relative error of at most 0.0073.
Values may be sent and summed in bfloat16 or wider, within the bound.
A program may use at most 64 MiB of HBM per device.

```python
import jax
import jax.numpy as jnp
from jax import lax

NZ = 64
TPL = 12
TVOX = 1728
O_DEV = 16
ORI = 64
NY = 16
NX = 32
N_ORI = 4


def template_rows(key):
    base_key = jax.random.fold_in(key, 71)
    raw_rows = jax.random.normal(base_key, (ORI, TVOX), jnp.float32)
    unit_rows = raw_rows / jnp.sqrt(jnp.sum(raw_rows * raw_rows, axis=1, keepdims=True))
    return unit_rows


def draw_templates(key, part):
    return template_rows(key).astype(jnp.bfloat16)


def draw_volume(key, part):
    noise_key = jax.random.fold_in(key, 3)
    volume = jax.random.normal(noise_key, (NY, NX, NZ), jnp.float32)
    return jnp.clip(volume, -1000.0, 1000.0)


def touch_ends(drawn, stream_key, low, largest):
    shape = drawn.shape
    index_at = [jax.random.randint(jax.random.fold_in(stream_key, axis), (), 0, shape[axis]) for axis in range(len(shape))]
    drawn = drawn.at[tuple(index_at)].set(low)
    longest = shape.index(max(shape))
    index_at[longest] = (index_at[longest] + 1) % shape[longest]
    return drawn.at[tuple(index_at)].set(largest)


def levels(own_key, shape, shards, least, largest):
    factor_of = 1.0
    for axis_at, blocks in shards:
        draws = jax.random.uniform(jax.random.fold_in(jax.random.fold_in(own_key, 6), axis_at), (blocks,), jnp.float32, least / len(shards), largest / len(shards))
        factor_of = factor_of * jnp.repeat(jnp.exp(draws), shape[axis_at] // blocks).reshape((-1,) + (1,) * (len(shape) - 1 - axis_at))
    return factor_of


def gaussian(rng, dims, scale, limit, cuts=(), dtype=jnp.bfloat16):
    drawn = scale * jax.random.normal(rng, dims, jnp.float32)
    if cuts:
        drawn = drawn * levels(rng, dims, cuts, -0.22, 0.18)
    return jnp.clip(drawn, -limit, limit).astype(dtype)


def setup_inputs(seed: int = 0, part: int = 0) -> dict:
    key_of = jax.random.split(jax.random.key(seed), 5)
    part_keys = jax.random.split(jax.random.fold_in(key_of[4], part), 5)
    volume = draw_volume(jax.random.fold_in(jax.random.fold_in(key_of[4], part), 71), part)
    templates = draw_templates(jax.random.fold_in(jax.random.fold_in(key_of[4], part), 71), part)
    prior_table = touch_ends(jax.random.randint(key_of[2], (ORI,), 0, 8), jax.random.fold_in(key_of[2], 1), 0, 7).astype(jnp.int32)
    moment_table = gaussian(key_of[3], (4, ORI), 1.0, 6.0, ((1, 4),), jnp.float32)
    return {"volume": volume, "templates": templates, "prior_table": prior_table, "moment_table": moment_table}


score_scale = 7.0
prior_step = 0.5
epsilon = 1e-05

def window_sums(values_in):
    tile_rows = values_in.shape[0] - 4
    tile_cols = values_in.shape[1] - 4
    z_cells = values_in.shape[2]
    padded = jnp.pad(values_in, ((0, 0), (0, 0), (2, 2)))
    along_z = padded[:, :, 0:z_cells]
    for offset in range(1, 5):
        along_z = along_z + padded[:, :, offset:offset + z_cells]
    along_x = along_z[:, 0:tile_cols]
    for offset in range(1, 5):
        along_x = along_x + along_z[:, offset:offset + tile_cols]
    along_y = along_x[0:tile_rows]
    for offset in range(1, 5):
        along_y = along_y + along_x[offset:offset + tile_rows]
    return along_y

def normalise(raw_ext):
    local_mean = window_sums(raw_ext) / 125.0
    second = window_sums(raw_ext * raw_ext) / 125.0
    spread = second - local_mean * local_mean
    centre = raw_ext[2:-2, 2:-2]
    return (centre - local_mean) * lax.rsqrt(spread + epsilon)

def reference(volume, templates, prior_table, moment_table):
    raw_ext = jnp.pad(volume, ((2, 2), (2, 2), (0, 0)))
    normed = lax.optimization_barrier(normalise(raw_ext).astype(jnp.bfloat16)).astype(jnp.float32)
    padded = jnp.pad(normed, ((5, 6), (5, 6), (5, 6)))[None, None]
    template_cubes = templates.astype(jnp.float32).reshape(N_ORI, O_DEV, 1, TPL, TPL, TPL)
    priors = (-prior_step * prior_table.astype(jnp.float32)).reshape(N_ORI, O_DEV)
    tables = moment_table.reshape(4, N_ORI, O_DEV).transpose(1, 0, 2)

    def merge_block(state_now, block_data):
        running_peak, running_total, firsts = state_now
        cube_block, prior_block, table_block = block_data
        correlation = lax.conv_general_dilated(padded, cube_block, (1, 1, 1), 'VALID', dimension_numbers=('NCDHW', 'OIDHW', 'NCDHW'), precision=lax.Precision.HIGHEST, preferred_element_type=jnp.float32)[0]
        scores = score_scale * correlation + prior_block[:, None, None, None]
        new_peak = jnp.maximum(running_peak, lax.optimization_barrier(jnp.max(scores, axis=0)))
        rescale = jnp.exp(running_peak - new_peak)
        exp_terms = jnp.exp(scores - new_peak[None])
        running_total = running_total * rescale + lax.optimization_barrier(jnp.sum(exp_terms, axis=0))
        firsts = firsts * rescale[None] + jnp.einsum('co,oyxz->cyxz', table_block, exp_terms, precision=lax.Precision.HIGHEST)
        return ((new_peak, running_total, firsts), None)
    start_state = (jnp.full((NY, NX, NZ), -1e+30, jnp.float32), jnp.zeros((NY, NX, NZ), jnp.float32), jnp.zeros((4, NY, NX, NZ), jnp.float32))
    final_state, _ = lax.scan(merge_block, start_state, (template_cubes, priors, tables))
    running_peak, running_total, firsts = final_state
    log_total = running_peak + jnp.log(running_total)
    moments = firsts / running_total[None]
    return (log_total, moments)
```

```python
import functools

import jax
import jax.numpy as jnp
from jax import lax
from jax.experimental import pallas as pl
from jax.experimental.pallas import tpu as pltpu
from jax.sharding import PartitionSpec as P

score_scale = 7.0
prior_step = 0.5
epsilon = 1e-05
MESH = pl.DeviceIdType.MESH
f32 = jnp.float32
bf16 = jnp.bfloat16
EDGE = 8
WIDE = 24


def iota(shape, dim):
    return lax.broadcasted_iota(jnp.int32, shape, dim)


def kernel(
    n_ori, n_ty, own,
    vol_ref, tmpl_ref, prior_ref, mom_ref, out_ref,
    ext, tall, aux, shifts, grid_ref, weights,
    vol_send, vol_recv, tmpl_send, tmpl_recv, aux_send, aux_recv,
):
    rows, cols, z_cells = vol_ref.shape
    orients = tmpl_ref.shape[0]
    all_orients = n_ori * orients
    ori = lax.axis_index("ori")
    ty = lax.axis_index("ty")
    tx = lax.axis_index("tx")
    has_prev = ty > 0
    has_next = ty < n_ty - 1
    other = 1 - tx
    pairs = (own + 1) // 2

    barrier = pltpu.get_barrier_semaphore()
    for k in range(1, n_ori):
        pl.semaphore_signal(
            barrier, inc=1, device_id={"ori": lax.rem(ori + k, n_ori)}, device_id_type=MESH
        )
    pl.semaphore_signal(barrier, inc=1, device_id={"tx": other}, device_id_type=MESH)

    @pl.when(has_prev)
    def _():
        pl.semaphore_signal(barrier, inc=1, device_id={"ty": ty - 1}, device_id_type=MESH)
        pl.semaphore_signal(
            barrier, inc=1, device_id={"ty": ty - 1, "tx": other}, device_id_type=MESH
        )

    @pl.when(has_next)
    def _():
        pl.semaphore_signal(barrier, inc=1, device_id={"ty": ty + 1}, device_id_type=MESH)
        pl.semaphore_signal(
            barrier, inc=1, device_id={"ty": ty + 1, "tx": other}, device_id_type=MESH
        )

    lanes = aux.shape[2]
    place = (iota((orients, lanes), 1) == iota((orients, lanes), 0) + ori * orients).astype(f32)
    small = jnp.concatenate(
        [mom_ref[...], prior_ref[...].astype(f32), jnp.zeros((3, orients), f32)], axis=0
    )
    aux[ori] = jnp.dot(small, place, precision=lax.Precision.HIGHEST, preferred_element_type=f32)
    own_cols = pl.ds(pl.multiple_of(EDGE + tx * cols, 8), cols)

    greeted = n_ori + jnp.where(has_prev, 2, 0) + jnp.where(has_next, 2, 0)
    pl.semaphore_wait(barrier, greeted)

    edge_src = pl.ds(pl.multiple_of((1 - tx) * (cols - 8), 8), 8)
    edge_dst = pl.ds(pl.multiple_of(EDGE + tx * cols + (1 - tx) * (cols - 8), 8), 8)

    def vol_copy(slot, whole, row, device):
        return pltpu.make_async_remote_copy(
            src_ref=vol_ref if whole else vol_ref.at[:, edge_src, :],
            dst_ref=ext.at[pl.ds(row, rows), own_cols if whole else edge_dst, :],
            send_sem=vol_send.at[slot],
            recv_sem=vol_recv.at[slot],
            device_id=device,
            device_id_type=MESH,
        )

    to_core = vol_copy(0, False, rows, {"tx": other})
    to_next = vol_copy(1, True, 0, {"ty": ty + 1})
    to_next_x = vol_copy(2, False, 0, {"ty": ty + 1, "tx": other})
    to_prev = vol_copy(3, True, 2 * rows, {"ty": ty - 1})
    to_prev_x = vol_copy(4, False, 2 * rows, {"ty": ty - 1, "tx": other})

    @pl.when(has_next)
    def _():
        to_next.start()
        to_next_x.start()

    @pl.when(has_prev)
    def _():
        to_prev.start()
        to_prev_x.start()

    to_core.start()
    gathers = []
    for k in sorted(range(1, n_ori), key=lambda k: -min(k, n_ori - k)):
        target = {"ori": lax.rem(ori + k, n_ori)}
        for src, dst, ssem, rsem in (
            (tmpl_ref, tall.at[ori], tmpl_send, tmpl_recv),
            (aux.at[ori], aux.at[ori], aux_send, aux_recv),
        ):
            copy = pltpu.make_async_remote_copy(
                src_ref=src, dst_ref=dst, send_sem=ssem.at[k - 1], recv_sem=rsem.at[k - 1],
                device_id=target, device_id_type=MESH,
            )
            copy.start()
            gathers.append(copy)

    tall[ori] = tmpl_ref[...]
    ext[pl.ds(rows, rows), own_cols, :] = vol_ref[...]
    edge = jnp.zeros((3 * rows, EDGE, z_cells), f32)
    ext[:, 0:EDGE, :] = edge
    ext[:, EDGE + 2 * cols : EDGE + 2 * cols + EDGE, :] = edge

    blank = jnp.zeros((rows, 2 * cols, z_cells), f32)

    @pl.when(jnp.logical_not(has_prev))
    def _():
        ext[0:rows, EDGE : EDGE + 2 * cols, :] = blank

    @pl.when(jnp.logical_not(has_next))
    def _():
        ext[2 * rows : 3 * rows, EDGE : EDGE + 2 * cols, :] = blank

    gap = iota((128, 128), 0) - iota((128, 128), 1)
    same = (iota((128, 128), 0) >= 64) == (iota((128, 128), 1) >= 64)
    for c in range(12):
        shifts[:, c * 128 : (c + 1) * 128] = ((gap == c - 5) & same).astype(f32).astype(bf16)
    row_id = iota((288, 384), 0)
    col_id = iota((288, 384), 1)
    half = jnp.where(col_id >= 192, 1, 0)
    within = col_id - 192 * half
    tap_b = within & 15
    perm = (
        (row_id == 144 * half + tap_b * 12 + (within >> 4)) & (tap_b < 12)
    ).astype(f32).astype(bf16)

    to_core.wait()

    @pl.when(has_next)
    def _():
        to_prev_in = vol_copy(3, True, 2 * rows, {"ty": ty + 1})
        to_prev_x_in = vol_copy(4, False, 2 * rows, {"ty": ty + 1, "tx": other})
        to_next.wait_send()
        to_next_x.wait_send()
        to_prev_in.wait_recv()
        to_prev_x_in.wait_recv()

    @pl.when(has_prev)
    def _():
        to_next_in = vol_copy(1, True, 0, {"ty": ty - 1})
        to_next_x_in = vol_copy(2, False, 0, {"ty": ty - 1, "tx": other})
        to_prev.wait_send()
        to_prev_x.wait_send()
        to_next_in.wait_recv()
        to_next_x_in.wait_recv()

    grid_rows = rows + 11
    x_first = tx * cols + ori * own
    raw = ext[1 : rows + 16, pl.ds(x_first + 1, WIDE), :]
    both = jnp.concatenate([raw, raw * raw], axis=-1)
    sums = both[0:grid_rows]
    for d in range(1, 5):
        sums = sums + both[d : d + grid_rows]
    flat = sums
    for d in range(1, 5):
        flat = flat + pltpu.roll(sums, WIDE - d, 1)
    lane = iota(flat.shape, 2) & 63
    total = flat
    for d in (1, 2):
        total = total + jnp.where(lane >= d, pltpu.roll(flat, d, 2), 0.0)
        total = total + jnp.where(lane < z_cells - d, pltpu.roll(flat, 128 - d, 2), 0.0)
    mean = total * (1.0 / 125.0)
    second = pltpu.roll(mean, 64, 2)
    centre = pltpu.roll(both[2 : 2 + grid_rows], WIDE - 2, 1)
    normed = (centre - mean) * lax.rsqrt(second - mean * mean + epsilon)
    y_at = iota(flat.shape, 0) + (ty * rows - 5)
    x_at = iota(flat.shape, 1)
    x_glob = x_at + (x_first - 5)
    inside = (y_at >= 0) & (y_at < n_ty * rows) & (x_glob >= 0) & (x_glob < 2 * cols)
    inside = inside & (x_at < own + 11) & (iota(flat.shape, 2) < z_cells)
    normed = jnp.where(inside, normed, 0.0).astype(bf16).astype(f32)
    blocks = []
    for p in range(pairs):
        block = normed[:, 2 * p : 2 * p + 16, :]
        if 2 * p + 1 < own:
            block = block + pltpu.roll(normed[:, 2 * p + 1 : 2 * p + 17, :], 64, 2)
        blocks.append(block.astype(bf16).reshape(grid_rows * 16, 128))
    stacked = jnp.concatenate(blocks, axis=0)
    for c in range(0, 12, 2):
        moved = jnp.dot(
            stacked, shifts[:, c * 128 : (c + 2) * 128], preferred_element_type=f32
        ).astype(bf16)
        for p in range(pairs):
            part = moved[p * grid_rows * 16 : (p + 1) * grid_rows * 16]
            for e in range(2):
                grid_ref[:, c + e, :, p * 128 : (p + 1) * 128] = part[
                    :, e * 128 : (e + 1) * 128
                ].reshape(grid_rows, 16, 128)

    for copy in gathers:
        copy.wait()
    cubes = tall[...].reshape(all_orients, 1728)
    for a in range(6):
        weights[:, a * 384 : (a + 1) * 384] = jnp.dot(
            cubes[:, a * 288 : (a + 1) * 288], perm, preferred_element_type=f32
        ).astype(bf16)
    table = jnp.sum(aux[...], axis=0)[:, 0:all_orients]
    eye = iota((all_orients, all_orients), 0) == iota((all_orients, all_orients), 1)
    prior = jnp.sum(jnp.where(eye, table[4:5], 0.0), axis=1, keepdims=True) * prior_step
    high = table[0:4].astype(bf16)
    low = (table[0:4] - high.astype(f32)).astype(bf16)
    factors = jnp.concatenate(
        [high.astype(f32), low.astype(f32), jnp.ones((8, all_orients), f32)], axis=0
    ).astype(bf16)
    for y in range(rows):
        window = grid_ref[y : y + 12].reshape(2304, pairs * 128)
        corr = jnp.dot(weights[...], window, preferred_element_type=f32)
        scores = score_scale * corr - prior
        peak = jnp.max(scores, axis=0, keepdims=True)
        terms = jnp.exp(scores - peak)
        log_total = peak + jnp.log(jnp.sum(terms, axis=0, keepdims=True))
        firsts = jnp.dot(factors, terms.astype(bf16), preferred_element_type=f32)
        out_ref[0, y : y + 1, :] = log_total
        moments = (firsts[0:4] + firsts[4:8]) / firsts[8:9]
        for k in range(4):
            out_ref[1 + k, y : y + 1, :] = moments[k : k + 1]


def shards(volume, templates, prior_table, moment_table):
    rows, cols, z_cells = volume.shape
    orients = templates.shape[0]
    n_ori = lax.axis_size("ori")
    n_ty = lax.axis_size("ty")
    own = cols // n_ori
    pairs = (own + 1) // 2
    lanes = max(128, n_ori * orients)
    vmem = pl.BlockSpec(memory_space=pltpu.VMEM)
    dma = pltpu.SemaphoreType.DMA
    out = pl.pallas_call(
        functools.partial(kernel, n_ori, n_ty, own),
        out_shape=jax.ShapeDtypeStruct((5, rows, pairs * 128), f32),
        in_specs=[vmem] * 4,
        out_specs=vmem,
        scratch_shapes=[
            pltpu.VMEM((3 * rows, 2 * cols + 3 * EDGE, z_cells), f32),
            pltpu.VMEM((n_ori, orients, 1728), bf16),
            pltpu.VMEM((n_ori, 8, lanes), f32),
            pltpu.VMEM((128, 12 * 128), bf16),
            pltpu.VMEM((rows + 11, 12, 16, pairs * 128), bf16),
            pltpu.VMEM((n_ori * orients, 2304), bf16),
            dma((5,)), dma((5,)),
            dma((n_ori - 1,)), dma((n_ori - 1,)),
            dma((n_ori - 1,)), dma((n_ori - 1,)),
        ],
        compiler_params=pltpu.CompilerParams(
            collective_id=0, has_side_effects=True, vmem_limit_bytes=48 * 2**20
        ),
    )(volume, templates, prior_table.reshape(1, orients), moment_table)
    out = out[:, :, : own * z_cells].reshape(5, rows, own, z_cells)
    return out[0], out[1:]


def solution(mesh):
    in_specs = (P(("grp", "ty"), "tx", None), P(("grp", "ori"), None), P("ori"), P(None, "ori"))
    out_specs = (P(("grp", "ty"), ("tx", "ori"), None), P(None, ("grp", "ty"), ("tx", "ori"), None))
    return jax.shard_map(shards, mesh=mesh, in_specs=in_specs, out_specs=out_specs, check_vma=False)
```

```python
import functools

import jax
import jax.numpy as jnp
from jax import lax
from jax.experimental import pallas as pl
from jax.experimental.pallas import tpu as pltpu
from jax.sharding import PartitionSpec as P

score_scale = 7.0
prior_step = 0.5
epsilon = 1e-05
MESH = pl.DeviceIdType.MESH
f32 = jnp.float32
bf16 = jnp.bfloat16
EDGE = 8
WIDE = 24


def iota(shape, dim):
    return lax.broadcasted_iota(jnp.int32, shape, dim)


def kernel(
    n_ori, n_ty, own,
    vol_ref, tmpl_ref, prior_ref, mom_ref, log_ref, mean_ref,
    ext, tall, aux, shifts, grid_ref, weights, prior_in, mom_in,
    local_sem,
    vol_send, vol_recv, tmpl_send, tmpl_recv, aux_send, aux_recv,
):
    rows, cols, z_cells = vol_ref.shape
    orients = tmpl_ref.shape[0]
    all_orients = n_ori * orients
    ori = lax.axis_index("ori")
    ty = lax.axis_index("ty")
    tx = lax.axis_index("tx")
    has_prev = ty > 0
    has_next = ty < n_ty - 1
    other = 1 - tx
    pairs = (own + 1) // 2
    own_cols = pl.ds(pl.multiple_of(EDGE + tx * cols, 8), cols)
    own_copies = [
        pltpu.make_async_copy(src, dst, local_sem.at[i])
        for i, (src, dst) in enumerate((
            (mom_ref, mom_in),
            (prior_ref, prior_in),
            (vol_ref, ext.at[pl.ds(rows, rows), own_cols, :]),
            (tmpl_ref, tall.at[ori]),
        ))
    ]

    barrier = pltpu.get_barrier_semaphore()
    for k in range(1, n_ori):
        pl.semaphore_signal(
            barrier, inc=1, device_id={"ori": lax.rem(ori + k, n_ori)}, device_id_type=MESH
        )
    pl.semaphore_signal(barrier, inc=1, device_id={"tx": other}, device_id_type=MESH)

    @pl.when(has_prev)
    def _():
        pl.semaphore_signal(barrier, inc=1, device_id={"ty": ty - 1}, device_id_type=MESH)
        pl.semaphore_signal(
            barrier, inc=1, device_id={"ty": ty - 1, "tx": other}, device_id_type=MESH
        )

    @pl.when(has_next)
    def _():
        pl.semaphore_signal(barrier, inc=1, device_id={"ty": ty + 1}, device_id_type=MESH)
        pl.semaphore_signal(
            barrier, inc=1, device_id={"ty": ty + 1, "tx": other}, device_id_type=MESH
        )

    for copy in own_copies:
        copy.start()
    lanes = aux.shape[2]
    place = (iota((orients, lanes), 1) == iota((orients, lanes), 0) + ori * orients).astype(f32)
    own_copies[0].wait()
    own_copies[1].wait()
    small = jnp.concatenate(
        [mom_in[...], prior_in[...].astype(f32), jnp.zeros((3, orients), f32)], axis=0
    )
    aux[ori] = jnp.dot(small, place, precision=lax.Precision.HIGHEST, preferred_element_type=f32)

    greeted = n_ori + jnp.where(has_prev, 2, 0) + jnp.where(has_next, 2, 0)
    pl.semaphore_wait(barrier, greeted)

    edge_src = pl.ds(pl.multiple_of((1 - tx) * (cols - 8), 8), 8)
    edge_dst = pl.ds(pl.multiple_of(EDGE + tx * cols + (1 - tx) * (cols - 8), 8), 8)

    def vol_copy(slot, whole, row, device):
        return pltpu.make_async_remote_copy(
            src_ref=vol_ref if whole else vol_ref.at[:, edge_src, :],
            dst_ref=ext.at[pl.ds(row, rows), own_cols if whole else edge_dst, :],
            send_sem=vol_send.at[slot],
            recv_sem=vol_recv.at[slot],
            device_id=device,
            device_id_type=MESH,
        )

    to_core = vol_copy(0, False, rows, {"tx": other})
    to_next = vol_copy(1, True, 0, {"ty": ty + 1})
    to_next_x = vol_copy(2, False, 0, {"ty": ty + 1, "tx": other})
    to_prev = vol_copy(3, True, 2 * rows, {"ty": ty - 1})
    to_prev_x = vol_copy(4, False, 2 * rows, {"ty": ty - 1, "tx": other})

    @pl.when(has_next)
    def _():
        to_next.start()
        to_next_x.start()

    @pl.when(has_prev)
    def _():
        to_prev.start()
        to_prev_x.start()

    to_core.start()
    gathers = []
    for k in sorted(range(1, n_ori), key=lambda k: -min(k, n_ori - k)):
        target = {"ori": lax.rem(ori + k, n_ori)}
        for src, dst, ssem, rsem in (
            (tmpl_ref, tall.at[ori], tmpl_send, tmpl_recv),
            (aux.at[ori], aux.at[ori], aux_send, aux_recv),
        ):
            copy = pltpu.make_async_remote_copy(
                src_ref=src, dst_ref=dst, send_sem=ssem.at[k - 1], recv_sem=rsem.at[k - 1],
                device_id=target, device_id_type=MESH,
            )
            copy.start()
            gathers.append(copy)

    edge = jnp.zeros((3 * rows, EDGE, z_cells), f32)
    ext[:, 0:EDGE, :] = edge
    ext[:, EDGE + 2 * cols : EDGE + 2 * cols + EDGE, :] = edge

    blank = jnp.zeros((rows, 2 * cols, z_cells), f32)

    @pl.when(jnp.logical_not(has_prev))
    def _():
        ext[0:rows, EDGE : EDGE + 2 * cols, :] = blank

    @pl.when(jnp.logical_not(has_next))
    def _():
        ext[2 * rows : 3 * rows, EDGE : EDGE + 2 * cols, :] = blank

    gap = iota((128, 128), 0) - iota((128, 128), 1)
    same = (iota((128, 128), 0) >= 64) == (iota((128, 128), 1) >= 64)
    for c in range(12):
        shifts[:, c * 128 : (c + 1) * 128] = ((gap == c - 5) & same).astype(f32).astype(bf16)
    row_id = iota((288, 384), 0)
    col_id = iota((288, 384), 1)
    half = jnp.where(col_id >= 192, 1, 0)
    within = col_id - 192 * half
    tap_b = within & 15
    perm = (
        (row_id == 144 * half + tap_b * 12 + (within >> 4)) & (tap_b < 12)
    ).astype(f32).astype(bf16)

    group = min(4, rows // 2)
    for g in range(group):
        band = slice(g * all_orients, (g + 1) * all_orients)
        if g:
            weights[band, 0 : g * 384] = jnp.zeros((all_orients, g * 384), bf16)
        if g < group - 1:
            weights[band, (6 + g) * 384 :] = jnp.zeros((all_orients, (group - 1 - g) * 384), bf16)
    own_copies[2].wait()
    own_copies[3].wait()
    to_core.wait()

    @pl.when(has_next)
    def _():
        to_prev_in = vol_copy(3, True, 2 * rows, {"ty": ty + 1})
        to_prev_x_in = vol_copy(4, False, 2 * rows, {"ty": ty + 1, "tx": other})
        to_next.wait_send()
        to_next_x.wait_send()
        to_prev_in.wait_recv()
        to_prev_x_in.wait_recv()

    @pl.when(has_prev)
    def _():
        to_next_in = vol_copy(1, True, 0, {"ty": ty - 1})
        to_next_x_in = vol_copy(2, False, 0, {"ty": ty - 1, "tx": other})
        to_prev.wait_send()
        to_prev_x.wait_send()
        to_next_in.wait_recv()
        to_next_x_in.wait_recv()

    grid_rows = rows + 11
    x_first = tx * cols + ori * own
    raw = ext[1 : rows + 16, pl.ds(x_first + 1, WIDE), :]
    both = jnp.concatenate([raw, raw * raw], axis=-1)
    sums = both[0:grid_rows]
    for d in range(1, 5):
        sums = sums + both[d : d + grid_rows]
    flat = sums
    for d in range(1, 5):
        flat = flat + pltpu.roll(sums, WIDE - d, 1)
    lane = iota(flat.shape, 2) & 63
    total = flat
    for d in (1, 2):
        total = total + jnp.where(lane >= d, pltpu.roll(flat, d, 2), 0.0)
        total = total + jnp.where(lane < z_cells - d, pltpu.roll(flat, 128 - d, 2), 0.0)
    mean = total * (1.0 / 125.0)
    second = pltpu.roll(mean, 64, 2)
    centre = pltpu.roll(both[2 : 2 + grid_rows], WIDE - 2, 1)
    normed = (centre - mean) * lax.rsqrt(second - mean * mean + epsilon)
    y_at = iota(flat.shape, 0) + (ty * rows - 5)
    x_at = iota(flat.shape, 1)
    x_glob = x_at + (x_first - 5)
    inside = (y_at >= 0) & (y_at < n_ty * rows) & (x_glob >= 0) & (x_glob < 2 * cols)
    inside = inside & (x_at < own + 11) & (iota(flat.shape, 2) < z_cells)
    normed = jnp.where(inside, normed, 0.0).astype(bf16).astype(f32)
    blocks = []
    for p in range(pairs):
        block = normed[:, 2 * p : 2 * p + 16, :]
        if 2 * p + 1 < own:
            block = block + pltpu.roll(normed[:, 2 * p + 1 : 2 * p + 17, :], 64, 2)
        blocks.append(block.astype(bf16).reshape(grid_rows * 16, 128))
    stacked = jnp.concatenate(blocks, axis=0)
    for c in range(0, 12, 2):
        moved = jnp.dot(
            stacked, shifts[:, c * 128 : (c + 2) * 128], preferred_element_type=f32
        ).astype(bf16)
        for p in range(pairs):
            part = moved[p * grid_rows * 16 : (p + 1) * grid_rows * 16]
            for e in range(2):
                grid_ref[:, c + e, :, p * 128 : (p + 1) * 128] = part[
                    :, e * 128 : (e + 1) * 128
                ].reshape(grid_rows, 16, 128)

    for copy in gathers:
        copy.wait()
    cubes = tall[...].reshape(all_orients, 1728)
    for a in range(6):
        tap = jnp.dot(
            cubes[:, a * 288 : (a + 1) * 288], perm, preferred_element_type=f32
        ).astype(bf16)
        for g in range(group):
            weights[g * all_orients : (g + 1) * all_orients, (a + g) * 384 : (a + g + 1) * 384] = tap
    table = jnp.sum(aux[...], axis=0)[:, 0:all_orients]
    eye = iota((all_orients, all_orients), 0) == iota((all_orients, all_orients), 1)
    prior = jnp.sum(jnp.where(eye, table[4:5], 0.0), axis=1, keepdims=True) * prior_step
    high = table[0:4].astype(bf16)
    low = (table[0:4] - high.astype(f32)).astype(bf16)
    factors = jnp.concatenate(
        [high.astype(f32), low.astype(f32), jnp.ones((8, all_orients), f32)], axis=0
    ).astype(bf16)
    depth = (2 * group + 10) * 192
    for first in range(0, rows, 2 * group):
        for start in (first, first + 1):
            window = grid_ref[start : start + 2 * group + 10].reshape(depth, pairs * 128)
            corr = jnp.dot(weights[...], window, preferred_element_type=f32)
            for g in range(group):
                y = start + 2 * g
                scores = score_scale * corr[g * all_orients : (g + 1) * all_orients] - prior
                peak = jnp.max(scores, axis=0, keepdims=True)
                terms = jnp.exp(scores - peak)
                log_total = peak + jnp.log(jnp.sum(terms, axis=0, keepdims=True))
                firsts = jnp.dot(factors, terms.astype(bf16), preferred_element_type=f32)
                moments = (firsts[0:4] + firsts[4:8]) / firsts[8:9]
                log_ref[y : y + 1, :] = log_total
                for k in range(4):
                    mean_ref[k, y : y + 1, :] = moments[k : k + 1]


def shards(volume, templates, prior_table, moment_table):
    rows, cols, z_cells = volume.shape
    orients = templates.shape[0]
    n_ori = lax.axis_size("ori")
    n_ty = lax.axis_size("ty")
    own = cols // n_ori
    pairs = (own + 1) // 2
    group = min(4, rows // 2)
    lanes = max(128, n_ori * orients)
    vmem = pl.BlockSpec(memory_space=pltpu.VMEM)
    dma = pltpu.SemaphoreType.DMA
    out = pl.pallas_call(
        functools.partial(kernel, n_ori, n_ty, own),
        out_shape=(
            jax.ShapeDtypeStruct((rows, pairs * 128), f32),
            jax.ShapeDtypeStruct((4, rows, pairs * 128), f32),
        ),
        in_specs=[pl.BlockSpec(memory_space=pltpu.HBM)] * 4,
        out_specs=(vmem, vmem),
        scratch_shapes=[
            pltpu.VMEM((3 * rows, 2 * cols + 3 * EDGE, z_cells), f32),
            pltpu.VMEM((n_ori, orients, 1728), bf16),
            pltpu.VMEM((n_ori, 8, lanes), f32),
            pltpu.VMEM((128, 12 * 128), bf16),
            pltpu.VMEM((rows + 11, 12, 16, pairs * 128), bf16),
            pltpu.VMEM((group * n_ori * orients, (2 * group + 10) * 192), bf16),
            pltpu.VMEM((1, orients), jnp.int32),
            pltpu.VMEM((4, orients), f32),
            dma((4,)),
            dma((5,)), dma((5,)),
            dma((n_ori - 1,)), dma((n_ori - 1,)),
            dma((n_ori - 1,)), dma((n_ori - 1,)),
        ],
        compiler_params=pltpu.CompilerParams(
            collective_id=0, has_side_effects=True, vmem_limit_bytes=60 * 2**20
        ),
    )(volume, templates, prior_table.reshape(1, orients), moment_table)
    return (
        out[0][:, : own * z_cells].reshape(rows, own, z_cells),
        out[1][:, :, : own * z_cells].reshape(4, rows, own, z_cells),
    )


def solution(mesh):
    in_specs = (P(("grp", "ty"), "tx", None), P(("grp", "ori"), None), P("ori"), P(None, "ori"))
    out_specs = (P(("grp", "ty"), ("tx", "ori"), None), P(None, ("grp", "ty"), ("tx", "ori"), None))
    return jax.shard_map(shards, mesh=mesh, in_specs=in_specs, out_specs=out_specs, check_vma=False)
```

```python
import functools

import jax
import jax.numpy as jnp
from jax import lax
from jax.experimental import pallas as pl
from jax.experimental.pallas import tpu as pltpu
from jax.sharding import PartitionSpec as P

score_scale = 7.0
prior_step = 0.5
epsilon = 1e-05
MESH = pl.DeviceIdType.MESH
f32 = jnp.float32
bf16 = jnp.bfloat16
EDGE = 8
WIDE = 24


def iota(shape, dim):
    return lax.broadcasted_iota(jnp.int32, shape, dim)


def kernel(
    n_ori, n_ty, own,
    vol_ref, tmpl_ref, prior_ref, mom_ref, log_ref, mean_ref,
    ext, tall, aux, shifts, grid_ref, weights, prior_in, mom_in,
    local_sem,
    vol_send, vol_recv, tmpl_send, tmpl_recv, aux_send, aux_recv, core_send, core_recv,
):
    rows, cols, z_cells = vol_ref.shape
    orients = tmpl_ref.shape[0]
    all_orients = n_ori * orients
    ori = lax.axis_index("ori")
    ty = lax.axis_index("ty")
    tx = lax.axis_index("tx")
    has_prev = ty > 0
    has_next = ty < n_ty - 1
    other = 1 - tx
    pairs = (own + 1) // 2
    own_cols = pl.ds(pl.multiple_of(EDGE + tx * cols, 8), cols)
    own_copies = [
        pltpu.make_async_copy(src, dst, local_sem.at[i])
        for i, (src, dst) in enumerate((
            (mom_ref, mom_in),
            (prior_ref, prior_in),
            (vol_ref, ext.at[pl.ds(rows, rows), own_cols, :]),
            (tmpl_ref, tall.at[ori]),
        ))
    ]

    barrier = pltpu.get_barrier_semaphore()
    for k in range(1, n_ori):
        pl.semaphore_signal(
            barrier, inc=1, device_id={"ori": lax.rem(ori + k, n_ori)}, device_id_type=MESH
        )
    pl.semaphore_signal(barrier, inc=1, device_id={"tx": other}, device_id_type=MESH)

    @pl.when(has_prev)
    def _():
        pl.semaphore_signal(barrier, inc=1, device_id={"ty": ty - 1}, device_id_type=MESH)
        pl.semaphore_signal(
            barrier, inc=1, device_id={"ty": ty - 1, "tx": other}, device_id_type=MESH
        )

    @pl.when(has_next)
    def _():
        pl.semaphore_signal(barrier, inc=1, device_id={"ty": ty + 1}, device_id_type=MESH)
        pl.semaphore_signal(
            barrier, inc=1, device_id={"ty": ty + 1, "tx": other}, device_id_type=MESH
        )

    for copy in own_copies:
        copy.start()
    lanes = aux.shape[2]
    place = (iota((orients, lanes), 1) == iota((orients, lanes), 0) + ori * orients).astype(f32)
    own_copies[0].wait()
    own_copies[1].wait()
    small = jnp.concatenate(
        [mom_in[...], prior_in[...].astype(f32), jnp.zeros((3, orients), f32)], axis=0
    )
    aux[ori] = jnp.dot(small, place, precision=lax.Precision.HIGHEST, preferred_element_type=f32)

    greeted = n_ori + jnp.where(has_prev, 2, 0) + jnp.where(has_next, 2, 0)
    pl.semaphore_wait(barrier, greeted)

    edge_src = pl.ds(pl.multiple_of((1 - tx) * (cols - 8), 8), 8)
    edge_dst = pl.ds(pl.multiple_of(EDGE + tx * cols + (1 - tx) * (cols - 8), 8), 8)

    def vol_copy(slot, whole, row, device):
        return pltpu.make_async_remote_copy(
            src_ref=vol_ref if whole else vol_ref.at[:, edge_src, :],
            dst_ref=ext.at[pl.ds(row, rows), own_cols if whole else edge_dst, :],
            send_sem=vol_send.at[slot],
            recv_sem=vol_recv.at[slot],
            device_id=device,
            device_id_type=MESH,
        )

    to_core = vol_copy(0, False, rows, {"tx": other})
    to_next = vol_copy(1, True, 0, {"ty": ty + 1})
    to_next_x = vol_copy(2, False, 0, {"ty": ty + 1, "tx": other})
    to_prev = vol_copy(3, True, 2 * rows, {"ty": ty - 1})
    to_prev_x = vol_copy(4, False, 2 * rows, {"ty": ty - 1, "tx": other})

    @pl.when(has_next)
    def _():
        to_next.start()
        to_next_x.start()

    @pl.when(has_prev)
    def _():
        to_prev.start()
        to_prev_x.start()

    to_core.start()
    gathers = []
    direct = []
    onward = []
    for k in range(1, n_ori):
        target = lax.rem(ori + k, n_ori)
        source = lax.rem(ori + n_ori - k, n_ori)
        direct.append((
            lax.rem(ori + target, 2) == tx,
            pltpu.make_async_remote_copy(
                src_ref=tmpl_ref, dst_ref=tall.at[ori], send_sem=tmpl_send.at[k - 1],
                recv_sem=tmpl_recv.at[k - 1], device_id={"ori": target}, device_id_type=MESH,
            ),
        ))
        onward.append((
            lax.rem(ori + source, 2) == tx,
            pltpu.make_async_remote_copy(
                src_ref=tmpl_ref, dst_ref=tall.at[source], send_sem=tmpl_send.at[k - 1],
                recv_sem=tmpl_recv.at[k - 1], device_id={"ori": source}, device_id_type=MESH,
            ),
            pltpu.make_async_remote_copy(
                src_ref=tall.at[source], dst_ref=tall.at[source], send_sem=core_send.at[k - 1],
                recv_sem=core_recv.at[k - 1], device_id={"tx": other}, device_id_type=MESH,
            ),
        ))
    for k in sorted(range(1, n_ori), key=lambda k: -min(k, n_ori - k)):
        pl.when(direct[k - 1][0])(direct[k - 1][1].start)
    for k in range(1, n_ori):
        copy = pltpu.make_async_remote_copy(
            src_ref=aux.at[ori], dst_ref=aux.at[ori], send_sem=aux_send.at[k - 1],
            recv_sem=aux_recv.at[k - 1], device_id={"ori": lax.rem(ori + k, n_ori)},
            device_id_type=MESH,
        )
        copy.start()
        gathers.append(copy)

    edge = jnp.zeros((3 * rows, EDGE, z_cells), f32)
    ext[:, 0:EDGE, :] = edge
    ext[:, EDGE + 2 * cols : EDGE + 2 * cols + EDGE, :] = edge

    blank = jnp.zeros((rows, 2 * cols, z_cells), f32)

    @pl.when(jnp.logical_not(has_prev))
    def _():
        ext[0:rows, EDGE : EDGE + 2 * cols, :] = blank

    @pl.when(jnp.logical_not(has_next))
    def _():
        ext[2 * rows : 3 * rows, EDGE : EDGE + 2 * cols, :] = blank

    gap = iota((128, 128), 0) - iota((128, 128), 1)
    same = (iota((128, 128), 0) >= 64) == (iota((128, 128), 1) >= 64)
    for c in range(12):
        shifts[:, c * 128 : (c + 1) * 128] = ((gap == c - 5) & same).astype(f32).astype(bf16)
    row_id = iota((288, 384), 0)
    col_id = iota((288, 384), 1)
    half = jnp.where(col_id >= 192, 1, 0)
    within = col_id - 192 * half
    tap_b = within & 15
    perm = (
        (row_id == 144 * half + tap_b * 12 + (within >> 4)) & (tap_b < 12)
    ).astype(f32).astype(bf16)

    group = min(4, rows // 2)
    for g in range(group):
        band = slice(g * all_orients, (g + 1) * all_orients)
        if g:
            weights[band, 0 : g * 384] = jnp.zeros((all_orients, g * 384), bf16)
        if g < group - 1:
            weights[band, (6 + g) * 384 :] = jnp.zeros((all_orients, (group - 1 - g) * 384), bf16)
    own_copies[2].wait()
    own_copies[3].wait()
    to_core.wait()

    @pl.when(has_next)
    def _():
        to_prev_in = vol_copy(3, True, 2 * rows, {"ty": ty + 1})
        to_prev_x_in = vol_copy(4, False, 2 * rows, {"ty": ty + 1, "tx": other})
        to_next.wait_send()
        to_next_x.wait_send()
        to_prev_in.wait_recv()
        to_prev_x_in.wait_recv()

    @pl.when(has_prev)
    def _():
        to_next_in = vol_copy(1, True, 0, {"ty": ty - 1})
        to_next_x_in = vol_copy(2, False, 0, {"ty": ty - 1, "tx": other})
        to_prev.wait_send()
        to_prev_x.wait_send()
        to_next_in.wait_recv()
        to_next_x_in.wait_recv()

    grid_rows = rows + 11
    x_first = tx * cols + ori * own
    raw = ext[1 : rows + 16, pl.ds(x_first + 1, WIDE), :]
    both = jnp.concatenate([raw, raw * raw], axis=-1)
    sums = both[0:grid_rows]
    for d in range(1, 5):
        sums = sums + both[d : d + grid_rows]
    flat = sums
    for d in range(1, 5):
        flat = flat + pltpu.roll(sums, WIDE - d, 1)
    lane = iota(flat.shape, 2) & 63
    total = flat
    for d in (1, 2):
        total = total + jnp.where(lane >= d, pltpu.roll(flat, d, 2), 0.0)
        total = total + jnp.where(lane < z_cells - d, pltpu.roll(flat, 128 - d, 2), 0.0)
    mean = total * (1.0 / 125.0)
    second = pltpu.roll(mean, 64, 2)
    centre = pltpu.roll(both[2 : 2 + grid_rows], WIDE - 2, 1)
    normed = (centre - mean) * lax.rsqrt(second - mean * mean + epsilon)
    y_at = iota(flat.shape, 0) + (ty * rows - 5)
    x_at = iota(flat.shape, 1)
    x_glob = x_at + (x_first - 5)
    inside = (y_at >= 0) & (y_at < n_ty * rows) & (x_glob >= 0) & (x_glob < 2 * cols)
    inside = inside & (x_at < own + 11) & (iota(flat.shape, 2) < z_cells)
    normed = jnp.where(inside, normed, 0.0).astype(bf16).astype(f32)
    for mine, arrival, forward in onward:

        @pl.when(mine)
        def _(arrival=arrival, forward=forward):
            arrival.wait_recv()
            forward.start()

    blocks = []
    for p in range(pairs):
        block = normed[:, 2 * p : 2 * p + 16, :]
        if 2 * p + 1 < own:
            block = block + pltpu.roll(normed[:, 2 * p + 1 : 2 * p + 17, :], 64, 2)
        blocks.append(block.astype(bf16).reshape(grid_rows * 16, 128))
    stacked = jnp.concatenate(blocks, axis=0)
    for c in range(0, 12, 2):
        moved = jnp.dot(
            stacked, shifts[:, c * 128 : (c + 2) * 128], preferred_element_type=f32
        ).astype(bf16)
        for p in range(pairs):
            part = moved[p * grid_rows * 16 : (p + 1) * grid_rows * 16]
            for e in range(2):
                grid_ref[:, c + e, :, p * 128 : (p + 1) * 128] = part[
                    :, e * 128 : (e + 1) * 128
                ].reshape(grid_rows, 16, 128)

    for copy in gathers:
        copy.wait()
    for leaves, copy in direct:
        pl.when(leaves)(copy.wait_send)
    for mine, arrival, forward in onward:
        pl.when(mine)(forward.wait_send)
        pl.when(jnp.logical_not(mine))(forward.wait_recv)
    cubes = tall[...].reshape(all_orients, 1728)
    for a in range(6):
        tap = jnp.dot(
            cubes[:, a * 288 : (a + 1) * 288], perm, preferred_element_type=f32
        ).astype(bf16)
        for g in range(group):
            weights[g * all_orients : (g + 1) * all_orients, (a + g) * 384 : (a + g + 1) * 384] = tap
    table = jnp.sum(aux[...], axis=0)[:, 0:all_orients]
    eye = iota((all_orients, all_orients), 0) == iota((all_orients, all_orients), 1)
    prior = jnp.sum(jnp.where(eye, table[4:5], 0.0), axis=1, keepdims=True) * prior_step
    high = table[0:4].astype(bf16)
    low = (table[0:4] - high.astype(f32)).astype(bf16)
    factors = jnp.concatenate(
        [high.astype(f32), low.astype(f32), jnp.ones((8, all_orients), f32)], axis=0
    ).astype(bf16)
    depth = (2 * group + 10) * 192
    for first in range(0, rows, 2 * group):
        for start in (first, first + 1):
            window = grid_ref[start : start + 2 * group + 10].reshape(depth, pairs * 128)
            corr = jnp.dot(weights[...], window, preferred_element_type=f32)
            for g in range(group):
                y = start + 2 * g
                scores = score_scale * corr[g * all_orients : (g + 1) * all_orients] - prior
                peak = jnp.max(scores, axis=0, keepdims=True)
                terms = jnp.exp(scores - peak)
                log_total = peak + jnp.log(jnp.sum(terms, axis=0, keepdims=True))
                firsts = jnp.dot(factors, terms.astype(bf16), preferred_element_type=f32)
                moments = (firsts[0:4] + firsts[4:8]) / firsts[8:9]
                log_ref[y : y + 1, :] = log_total
                for k in range(4):
                    mean_ref[k, y : y + 1, :] = moments[k : k + 1]


def shards(volume, templates, prior_table, moment_table):
    rows, cols, z_cells = volume.shape
    orients = templates.shape[0]
    n_ori = lax.axis_size("ori")
    n_ty = lax.axis_size("ty")
    own = cols // n_ori
    pairs = (own + 1) // 2
    group = min(4, rows // 2)
    lanes = max(128, n_ori * orients)
    vmem = pl.BlockSpec(memory_space=pltpu.VMEM)
    dma = pltpu.SemaphoreType.DMA
    out = pl.pallas_call(
        functools.partial(kernel, n_ori, n_ty, own),
        out_shape=(
            jax.ShapeDtypeStruct((rows, pairs * 128), f32),
            jax.ShapeDtypeStruct((4, rows, pairs * 128), f32),
        ),
        in_specs=[pl.BlockSpec(memory_space=pltpu.HBM)] * 4,
        out_specs=(vmem, vmem),
        scratch_shapes=[
            pltpu.VMEM((3 * rows, 2 * cols + 3 * EDGE, z_cells), f32),
            pltpu.VMEM((n_ori, orients, 1728), bf16),
            pltpu.VMEM((n_ori, 8, lanes), f32),
            pltpu.VMEM((128, 12 * 128), bf16),
            pltpu.VMEM((rows + 11, 12, 16, pairs * 128), bf16),
            pltpu.VMEM((group * n_ori * orients, (2 * group + 10) * 192), bf16),
            pltpu.VMEM((1, orients), jnp.int32),
            pltpu.VMEM((4, orients), f32),
            dma((4,)),
            dma((5,)), dma((5,)),
            dma((n_ori - 1,)), dma((n_ori - 1,)),
            dma((n_ori - 1,)), dma((n_ori - 1,)),
            dma((n_ori - 1,)), dma((n_ori - 1,)),
        ],
        compiler_params=pltpu.CompilerParams(
            collective_id=0, has_side_effects=True, vmem_limit_bytes=60 * 2**20
        ),
    )(volume, templates, prior_table.reshape(1, orients), moment_table)
    return (
        out[0][:, : own * z_cells].reshape(rows, own, z_cells),
        out[1][:, :, : own * z_cells].reshape(4, rows, own, z_cells),
    )


def solution(mesh):
    in_specs = (P(("grp", "ty"), "tx", None), P(("grp", "ori"), None), P("ori"), P(None, "ori"))
    out_specs = (P(("grp", "ty"), ("tx", "ori"), None), P(None, ("grp", "ty"), ("tx", "ori"), None))
    return jax.shard_map(shards, mesh=mesh, in_specs=in_specs, out_specs=out_specs, check_vma=False)
```

```python
import functools

import jax
import jax.numpy as jnp
from jax import lax
from jax.experimental import pallas as pl
from jax.experimental.pallas import tpu as pltpu
from jax.sharding import PartitionSpec as P

score_scale = 7.0
prior_step = 0.5
epsilon = 1e-05
MESH = pl.DeviceIdType.MESH
f32 = jnp.float32
bf16 = jnp.bfloat16
EDGE = 8
WIDE = 24


def iota(shape, dim):
    return lax.broadcasted_iota(jnp.int32, shape, dim)


def kernel(
    n_ori, n_ty, own,
    vol_ref, tmpl_ref, prior_ref, mom_ref, log_ref, mean_ref,
    ext, tall, aux, shifts, grid_ref, weights, prior_in, mom_in,
    local_sem,
    vol_send, vol_recv, tmpl_send, tmpl_recv, aux_send, aux_recv, core_send, core_recv,
):
    rows, cols, z_cells = vol_ref.shape
    orients = tmpl_ref.shape[0]
    all_orients = n_ori * orients
    ori = lax.axis_index("ori")
    ty = lax.axis_index("ty")
    tx = lax.axis_index("tx")
    has_prev = ty > 0
    has_next = ty < n_ty - 1
    other = 1 - tx
    pairs = (own + 1) // 2
    own_cols = pl.ds(pl.multiple_of(EDGE + tx * cols, 8), cols)
    own_copies = [
        pltpu.make_async_copy(src, dst, local_sem.at[i])
        for i, (src, dst) in enumerate((
            (mom_ref, mom_in),
            (prior_ref, prior_in),
            (vol_ref, ext.at[pl.ds(rows, rows), own_cols, :]),
            (tmpl_ref, tall.at[ori]),
        ))
    ]

    barrier = pltpu.get_barrier_semaphore()
    for k in range(1, n_ori):
        pl.semaphore_signal(
            barrier, inc=1, device_id={"ori": lax.rem(ori + k, n_ori)}, device_id_type=MESH
        )
    pl.semaphore_signal(barrier, inc=1, device_id={"tx": other}, device_id_type=MESH)

    @pl.when(has_prev)
    def _():
        pl.semaphore_signal(barrier, inc=1, device_id={"ty": ty - 1}, device_id_type=MESH)
        pl.semaphore_signal(
            barrier, inc=1, device_id={"ty": ty - 1, "tx": other}, device_id_type=MESH
        )

    @pl.when(has_next)
    def _():
        pl.semaphore_signal(barrier, inc=1, device_id={"ty": ty + 1}, device_id_type=MESH)
        pl.semaphore_signal(
            barrier, inc=1, device_id={"ty": ty + 1, "tx": other}, device_id_type=MESH
        )

    for copy in own_copies:
        copy.start()
    lanes = aux.shape[2]
    place = (iota((orients, lanes), 1) == iota((orients, lanes), 0) + ori * orients).astype(f32)
    own_copies[0].wait()
    own_copies[1].wait()
    small = jnp.concatenate(
        [mom_in[...], prior_in[...].astype(f32), jnp.zeros((3, orients), f32)], axis=0
    )
    aux[ori] = jnp.dot(small, place, precision=lax.Precision.HIGHEST, preferred_element_type=f32)

    greeted = n_ori + jnp.where(has_prev, 2, 0) + jnp.where(has_next, 2, 0)
    pl.semaphore_wait(barrier, greeted)

    edge_src = pl.ds(pl.multiple_of((1 - tx) * (cols - 8), 8), 8)
    edge_dst = pl.ds(pl.multiple_of(EDGE + tx * cols + (1 - tx) * (cols - 8), 8), 8)

    def vol_copy(slot, whole, row, device):
        return pltpu.make_async_remote_copy(
            src_ref=vol_ref if whole else vol_ref.at[:, edge_src, :],
            dst_ref=ext.at[pl.ds(row, rows), own_cols if whole else edge_dst, :],
            send_sem=vol_send.at[slot],
            recv_sem=vol_recv.at[slot],
            device_id=device,
            device_id_type=MESH,
        )

    to_core = vol_copy(0, False, rows, {"tx": other})
    to_next = vol_copy(1, True, 0, {"ty": ty + 1})
    to_next_x = vol_copy(2, False, 0, {"ty": ty + 1, "tx": other})
    to_prev = vol_copy(3, True, 2 * rows, {"ty": ty - 1})
    to_prev_x = vol_copy(4, False, 2 * rows, {"ty": ty - 1, "tx": other})

    @pl.when(has_next)
    def _():
        to_next.start()
        to_next_x.start()

    @pl.when(has_prev)
    def _():
        to_prev.start()
        to_prev_x.start()

    to_core.start()
    gathers = []
    direct = []
    onward = []
    for k in range(1, n_ori):
        target = lax.rem(ori + k, n_ori)
        source = lax.rem(ori + n_ori - k, n_ori)
        direct.append((
            lax.rem(ori + target, 2) == tx,
            pltpu.make_async_remote_copy(
                src_ref=tmpl_ref, dst_ref=tall.at[ori], send_sem=tmpl_send.at[k - 1],
                recv_sem=tmpl_recv.at[k - 1], device_id={"ori": target}, device_id_type=MESH,
            ),
        ))
        onward.append((
            lax.rem(ori + source, 2) == tx,
            pltpu.make_async_remote_copy(
                src_ref=tmpl_ref, dst_ref=tall.at[source], send_sem=tmpl_send.at[k - 1],
                recv_sem=tmpl_recv.at[k - 1], device_id={"ori": source}, device_id_type=MESH,
            ),
            pltpu.make_async_remote_copy(
                src_ref=tall.at[source], dst_ref=tall.at[source], send_sem=core_send.at[k - 1],
                recv_sem=core_recv.at[k - 1], device_id={"tx": other}, device_id_type=MESH,
            ),
        ))
    for k in sorted(range(1, n_ori), key=lambda k: -min(k, n_ori - k)):
        pl.when(direct[k - 1][0])(direct[k - 1][1].start)
    for k in range(1, n_ori):
        copy = pltpu.make_async_remote_copy(
            src_ref=aux.at[ori], dst_ref=aux.at[ori], send_sem=aux_send.at[k - 1],
            recv_sem=aux_recv.at[k - 1], device_id={"ori": lax.rem(ori + k, n_ori)},
            device_id_type=MESH,
        )
        copy.start()
        gathers.append(copy)

    edge = jnp.zeros((3 * rows, EDGE, z_cells), f32)
    ext[:, 0:EDGE, :] = edge
    ext[:, EDGE + 2 * cols : EDGE + 2 * cols + EDGE, :] = edge

    blank = jnp.zeros((rows, 2 * cols, z_cells), f32)

    @pl.when(jnp.logical_not(has_prev))
    def _():
        ext[0:rows, EDGE : EDGE + 2 * cols, :] = blank

    @pl.when(jnp.logical_not(has_next))
    def _():
        ext[2 * rows : 3 * rows, EDGE : EDGE + 2 * cols, :] = blank

    gap = iota((128, 128), 0) - iota((128, 128), 1)
    same = (iota((128, 128), 0) >= 64) == (iota((128, 128), 1) >= 64)
    for c in range(12):
        shifts[:, c * 128 : (c + 1) * 128] = ((gap == c - 5) & same).astype(f32).astype(bf16)
    row_id = iota((288, 384), 0)
    col_id = iota((288, 384), 1)
    half = jnp.where(col_id >= 192, 1, 0)
    within = col_id - 192 * half
    tap_b = within & 15
    perm = (
        (row_id == 144 * half + tap_b * 12 + (within >> 4)) & (tap_b < 12)
    ).astype(f32).astype(bf16)

    group = min(2, rows // 2)
    for g in range(group):
        band = slice(g * all_orients, (g + 1) * all_orients)
        if g:
            weights[band, 0 : g * 384] = jnp.zeros((all_orients, g * 384), bf16)
        if g < group - 1:
            weights[band, (6 + g) * 384 :] = jnp.zeros((all_orients, (group - 1 - g) * 384), bf16)
    own_copies[2].wait()
    own_copies[3].wait()
    to_core.wait()

    @pl.when(has_next)
    def _():
        to_prev_in = vol_copy(3, True, 2 * rows, {"ty": ty + 1})
        to_prev_x_in = vol_copy(4, False, 2 * rows, {"ty": ty + 1, "tx": other})
        to_next.wait_send()
        to_next_x.wait_send()
        to_prev_in.wait_recv()
        to_prev_x_in.wait_recv()

    @pl.when(has_prev)
    def _():
        to_next_in = vol_copy(1, True, 0, {"ty": ty - 1})
        to_next_x_in = vol_copy(2, False, 0, {"ty": ty - 1, "tx": other})
        to_prev.wait_send()
        to_prev_x.wait_send()
        to_next_in.wait_recv()
        to_next_x_in.wait_recv()

    for mine, arrival, forward in onward:

        @pl.when(mine)
        def _(arrival=arrival, forward=forward):
            arrival.wait_recv()
            forward.start()

    grid_rows = rows + 11
    x_first = tx * cols + ori * own
    raw = ext[1 : rows + 16, pl.ds(x_first + 1, WIDE), :]
    both = jnp.concatenate([raw, raw * raw], axis=-1)
    sums = both[0:grid_rows]
    for d in range(1, 5):
        sums = sums + both[d : d + grid_rows]
    flat = sums
    for d in range(1, 5):
        flat = flat + pltpu.roll(sums, WIDE - d, 1)
    lane = iota(flat.shape, 2) & 63
    total = flat
    for d in (1, 2):
        total = total + jnp.where(lane >= d, pltpu.roll(flat, d, 2), 0.0)
        total = total + jnp.where(lane < z_cells - d, pltpu.roll(flat, 128 - d, 2), 0.0)
    mean = total * (1.0 / 125.0)
    second = pltpu.roll(mean, 64, 2)
    centre = pltpu.roll(both[2 : 2 + grid_rows], WIDE - 2, 1)
    normed = (centre - mean) * lax.rsqrt(second - mean * mean + epsilon)
    y_at = iota(flat.shape, 0) + (ty * rows - 5)
    x_at = iota(flat.shape, 1)
    x_glob = x_at + (x_first - 5)
    inside = (y_at >= 0) & (y_at < n_ty * rows) & (x_glob >= 0) & (x_glob < 2 * cols)
    inside = inside & (x_at < own + 11) & (iota(flat.shape, 2) < z_cells)
    normed = jnp.where(inside, normed, 0.0).astype(bf16).astype(f32)
    blocks = []
    for p in range(pairs):
        block = normed[:, 2 * p : 2 * p + 16, :]
        if 2 * p + 1 < own:
            block = block + pltpu.roll(normed[:, 2 * p + 1 : 2 * p + 17, :], 64, 2)
        blocks.append(block.astype(bf16).reshape(grid_rows * 16, 128))
    stacked = jnp.concatenate(blocks, axis=0)
    for c in range(0, 12, 2):
        moved = jnp.dot(
            stacked, shifts[:, c * 128 : (c + 2) * 128], preferred_element_type=f32
        ).astype(bf16)
        for p in range(pairs):
            part = moved[p * grid_rows * 16 : (p + 1) * grid_rows * 16]
            for e in range(2):
                grid_ref[:, c + e, :, p * 128 : (p + 1) * 128] = part[
                    :, e * 128 : (e + 1) * 128
                ].reshape(grid_rows, 16, 128)

    for copy in gathers:
        copy.wait()
    for leaves, copy in direct:
        pl.when(leaves)(copy.wait_send)
    for mine, arrival, forward in onward:
        pl.when(mine)(forward.wait_send)
        pl.when(jnp.logical_not(mine))(forward.wait_recv)
    cubes = tall[...].reshape(all_orients, 1728)
    for a in range(6):
        tap = jnp.dot(
            cubes[:, a * 288 : (a + 1) * 288], perm, preferred_element_type=f32
        ).astype(bf16)
        for g in range(group):
            weights[g * all_orients : (g + 1) * all_orients, (a + g) * 384 : (a + g + 1) * 384] = tap
    table = jnp.sum(aux[...], axis=0)[:, 0:all_orients]
    eye = iota((all_orients, all_orients), 0) == iota((all_orients, all_orients), 1)
    prior = jnp.sum(jnp.where(eye, table[4:5], 0.0), axis=1, keepdims=True) * prior_step
    high = table[0:4].astype(bf16)
    low = (table[0:4] - high.astype(f32)).astype(bf16)
    factors = jnp.concatenate(
        [high.astype(f32), low.astype(f32), jnp.ones((8, all_orients), f32)], axis=0
    ).astype(bf16)
    depth = (2 * group + 10) * 192
    for first in range(0, rows, 2 * group):
        for start in (first, first + 1):
            window = grid_ref[start : start + 2 * group + 10].reshape(depth, pairs * 128)
            corr = jnp.dot(weights[...], window, preferred_element_type=f32)
            for g in range(group):
                y = start + 2 * g
                scores = score_scale * corr[g * all_orients : (g + 1) * all_orients] - prior
                peak = jnp.max(scores, axis=0, keepdims=True)
                terms = jnp.exp(scores - peak)
                log_total = peak + jnp.log(jnp.sum(terms, axis=0, keepdims=True))
                firsts = jnp.dot(factors, terms.astype(bf16), preferred_element_type=f32)
                moments = (firsts[0:4] + firsts[4:8]) / firsts[8:9]
                log_ref[y : y + 1, :] = log_total
                for k in range(4):
                    mean_ref[k, y : y + 1, :] = moments[k : k + 1]


def shards(volume, templates, prior_table, moment_table):
    rows, cols, z_cells = volume.shape
    orients = templates.shape[0]
    n_ori = lax.axis_size("ori")
    n_ty = lax.axis_size("ty")
    own = cols // n_ori
    pairs = (own + 1) // 2
    group = min(2, rows // 2)
    lanes = max(128, n_ori * orients)
    vmem = pl.BlockSpec(memory_space=pltpu.VMEM)
    dma = pltpu.SemaphoreType.DMA
    out = pl.pallas_call(
        functools.partial(kernel, n_ori, n_ty, own),
        out_shape=(
            jax.ShapeDtypeStruct((rows, pairs * 128), f32),
            jax.ShapeDtypeStruct((4, rows, pairs * 128), f32),
        ),
        in_specs=[pl.BlockSpec(memory_space=pltpu.HBM)] * 4,
        out_specs=(vmem, vmem),
        scratch_shapes=[
            pltpu.VMEM((3 * rows, 2 * cols + 3 * EDGE, z_cells), f32),
            pltpu.VMEM((n_ori, orients, 1728), bf16),
            pltpu.VMEM((n_ori, 8, lanes), f32),
            pltpu.VMEM((128, 12 * 128), bf16),
            pltpu.VMEM((rows + 11, 12, 16, pairs * 128), bf16),
            pltpu.VMEM((group * n_ori * orients, (2 * group + 10) * 192), bf16),
            pltpu.VMEM((1, orients), jnp.int32),
            pltpu.VMEM((4, orients), f32),
            dma((4,)),
            dma((5,)), dma((5,)),
            dma((n_ori - 1,)), dma((n_ori - 1,)),
            dma((n_ori - 1,)), dma((n_ori - 1,)),
            dma((n_ori - 1,)), dma((n_ori - 1,)),
        ],
        compiler_params=pltpu.CompilerParams(
            collective_id=0, has_side_effects=True, vmem_limit_bytes=55160 * 1024
        ),
    )(volume, templates, prior_table.reshape(1, orients), moment_table)
    return (
        out[0][:, : own * z_cells].reshape(rows, own, z_cells),
        out[1][:, :, : own * z_cells].reshape(4, rows, own, z_cells),
    )


def solution(mesh):
    in_specs = (P(("grp", "ty"), "tx", None), P(("grp", "ori"), None), P("ori"), P(None, "ori"))
    out_specs = (P(("grp", "ty"), ("tx", "ori"), None), P(None, ("grp", "ty"), ("tx", "ori"), None))
    return jax.shard_map(shards, mesh=mesh, in_specs=in_specs, out_specs=out_specs, check_vma=False)
```

```python
import functools

import jax
import jax.numpy as jnp
from jax import lax
from jax.experimental import pallas as pl
from jax.experimental.pallas import tpu as pltpu
from jax.sharding import PartitionSpec as P

score_scale = 7.0
prior_step = 0.5
epsilon = 1e-05
MESH = pl.DeviceIdType.MESH
f32 = jnp.float32
bf16 = jnp.bfloat16
EDGE = 8
WIDE = 24


def iota(shape, dim):
    return lax.broadcasted_iota(jnp.int32, shape, dim)


def kernel(
    n_ori, n_ty, own,
    vol_ref, tmpl_ref, prior_ref, mom_ref, log_ref, mean_ref,
    ext, tall, aux, shifts, grid_ref, weights, prior_in, mom_in,
    local_sem,
    vol_send, vol_recv, tmpl_send, tmpl_recv, aux_send, aux_recv, core_send, core_recv,
):
    rows, cols, z_cells = vol_ref.shape
    orients = tmpl_ref.shape[0]
    all_orients = n_ori * orients
    ori = lax.axis_index("ori")
    ty = lax.axis_index("ty")
    tx = lax.axis_index("tx")
    has_prev = ty > 0
    has_next = ty < n_ty - 1
    other = 1 - tx
    pairs = (own + 1) // 2
    own_cols = pl.ds(pl.multiple_of(EDGE + tx * cols, 8), cols)
    own_copies = [
        pltpu.make_async_copy(src, dst, local_sem.at[i])
        for i, (src, dst) in enumerate((
            (mom_ref, mom_in),
            (prior_ref, prior_in),
            (vol_ref, ext.at[pl.ds(rows, rows), own_cols, :]),
            (tmpl_ref, tall.at[ori]),
        ))
    ]

    barrier = pltpu.get_barrier_semaphore()
    for k in range(1, n_ori):
        pl.semaphore_signal(
            barrier, inc=1, device_id={"ori": lax.rem(ori + k, n_ori)}, device_id_type=MESH
        )
    pl.semaphore_signal(barrier, inc=1, device_id={"tx": other}, device_id_type=MESH)

    @pl.when(has_prev)
    def _():
        pl.semaphore_signal(barrier, inc=1, device_id={"ty": ty - 1}, device_id_type=MESH)
        pl.semaphore_signal(
            barrier, inc=1, device_id={"ty": ty - 1, "tx": other}, device_id_type=MESH
        )

    @pl.when(has_next)
    def _():
        pl.semaphore_signal(barrier, inc=1, device_id={"ty": ty + 1}, device_id_type=MESH)
        pl.semaphore_signal(
            barrier, inc=1, device_id={"ty": ty + 1, "tx": other}, device_id_type=MESH
        )

    for copy in own_copies:
        copy.start()
    lanes = aux.shape[2]
    place = (iota((orients, lanes), 1) == iota((orients, lanes), 0) + ori * orients).astype(f32)
    own_copies[0].wait()
    own_copies[1].wait()
    small = jnp.concatenate(
        [mom_in[...], prior_in[...].astype(f32), jnp.zeros((3, orients), f32)], axis=0
    )
    aux[ori] = jnp.dot(small, place, precision=lax.Precision.HIGHEST, preferred_element_type=f32)

    greeted = n_ori + jnp.where(has_prev, 2, 0) + jnp.where(has_next, 2, 0)
    pl.semaphore_wait(barrier, greeted)

    edge_src = pl.ds(pl.multiple_of((1 - tx) * (cols - 8), 8), 8)
    edge_dst = pl.ds(pl.multiple_of(EDGE + tx * cols + (1 - tx) * (cols - 8), 8), 8)

    def vol_copy(slot, whole, row, device):
        return pltpu.make_async_remote_copy(
            src_ref=vol_ref if whole else vol_ref.at[:, edge_src, :],
            dst_ref=ext.at[pl.ds(row, rows), own_cols if whole else edge_dst, :],
            send_sem=vol_send.at[slot],
            recv_sem=vol_recv.at[slot],
            device_id=device,
            device_id_type=MESH,
        )

    to_core = vol_copy(0, False, rows, {"tx": other})
    to_next = vol_copy(1, True, 0, {"ty": ty + 1})
    to_next_x = vol_copy(2, False, 0, {"ty": ty + 1, "tx": other})
    to_prev = vol_copy(3, True, 2 * rows, {"ty": ty - 1})
    to_prev_x = vol_copy(4, False, 2 * rows, {"ty": ty - 1, "tx": other})

    @pl.when(has_next)
    def _():
        to_next.start()
        to_next_x.start()

    @pl.when(has_prev)
    def _():
        to_prev.start()
        to_prev_x.start()

    to_core.start()
    gathers = []
    direct = []
    onward = []
    for k in range(1, n_ori):
        target = lax.rem(ori + k, n_ori)
        source = lax.rem(ori + n_ori - k, n_ori)
        direct.append((
            lax.rem(ori + target, 2) == tx,
            pltpu.make_async_remote_copy(
                src_ref=tmpl_ref, dst_ref=tall.at[ori], send_sem=tmpl_send.at[k - 1],
                recv_sem=tmpl_recv.at[k - 1], device_id={"ori": target}, device_id_type=MESH,
            ),
        ))
        onward.append((
            lax.rem(ori + source, 2) == tx,
            pltpu.make_async_remote_copy(
                src_ref=tmpl_ref, dst_ref=tall.at[source], send_sem=tmpl_send.at[k - 1],
                recv_sem=tmpl_recv.at[k - 1], device_id={"ori": source}, device_id_type=MESH,
            ),
            pltpu.make_async_remote_copy(
                src_ref=tall.at[source], dst_ref=tall.at[source], send_sem=core_send.at[k - 1],
                recv_sem=core_recv.at[k - 1], device_id={"tx": other}, device_id_type=MESH,
            ),
        ))
    for k in sorted(range(1, n_ori), key=lambda k: -min(k, n_ori - k)):
        pl.when(direct[k - 1][0])(direct[k - 1][1].start)
    for k in range(1, n_ori):
        copy = pltpu.make_async_remote_copy(
            src_ref=aux.at[ori], dst_ref=aux.at[ori], send_sem=aux_send.at[k - 1],
            recv_sem=aux_recv.at[k - 1], device_id={"ori": lax.rem(ori + k, n_ori)},
            device_id_type=MESH,
        )
        copy.start()
        gathers.append(copy)

    edge = jnp.zeros((3 * rows, EDGE, z_cells), f32)
    ext[:, 0:EDGE, :] = edge
    ext[:, EDGE + 2 * cols : EDGE + 2 * cols + EDGE, :] = edge

    blank = jnp.zeros((rows, 2 * cols, z_cells), f32)

    @pl.when(jnp.logical_not(has_prev))
    def _():
        ext[0:rows, EDGE : EDGE + 2 * cols, :] = blank

    @pl.when(jnp.logical_not(has_next))
    def _():
        ext[2 * rows : 3 * rows, EDGE : EDGE + 2 * cols, :] = blank

    gap = iota((128, 128), 0) - iota((128, 128), 1)
    same = (iota((128, 128), 0) >= 64) == (iota((128, 128), 1) >= 64)
    for c in range(12):
        shifts[:, c * 128 : (c + 1) * 128] = ((gap == c - 5) & same).astype(f32).astype(bf16)
    row_id = iota((288, 384), 0)
    col_id = iota((288, 384), 1)
    half = jnp.where(col_id >= 192, 1, 0)
    within = col_id - 192 * half
    tap_b = within & 15
    perm = (
        (row_id == 144 * half + tap_b * 12 + (within >> 4)) & (tap_b < 12)
    ).astype(f32).astype(bf16)

    group = min(2, rows // 2)
    for g in range(group):
        band = slice(g * all_orients, (g + 1) * all_orients)
        if g:
            weights[band, 0 : g * 384] = jnp.zeros((all_orients, g * 384), bf16)
        if g < group - 1:
            weights[band, (6 + g) * 384 :] = jnp.zeros((all_orients, (group - 1 - g) * 384), bf16)
    own_copies[2].wait()
    own_copies[3].wait()
    to_core.wait()

    @pl.when(has_next)
    def _():
        to_prev_in = vol_copy(3, True, 2 * rows, {"ty": ty + 1})
        to_prev_x_in = vol_copy(4, False, 2 * rows, {"ty": ty + 1, "tx": other})
        to_next.wait_send()
        to_next_x.wait_send()
        to_prev_in.wait_recv()
        to_prev_x_in.wait_recv()

    @pl.when(has_prev)
    def _():
        to_next_in = vol_copy(1, True, 0, {"ty": ty - 1})
        to_next_x_in = vol_copy(2, False, 0, {"ty": ty - 1, "tx": other})
        to_prev.wait_send()
        to_prev_x.wait_send()
        to_next_in.wait_recv()
        to_next_x_in.wait_recv()

    for mine, arrival, forward in onward:

        @pl.when(mine)
        def _(arrival=arrival, forward=forward):
            arrival.wait_recv()
            forward.start()

    grid_rows = rows + 11
    x_first = tx * cols + ori * own
    raw = ext[1 : rows + 16, pl.ds(x_first + 1, WIDE), :]
    both = jnp.concatenate([raw, raw * raw], axis=-1)
    sums = both[0:grid_rows]
    for d in range(1, 5):
        sums = sums + both[d : d + grid_rows]
    flat = sums
    for d in range(1, 5):
        flat = flat + pltpu.roll(sums, WIDE - d, 1)
    lane = iota(flat.shape, 2) & 63
    total = flat
    for d in (1, 2):
        total = total + jnp.where(lane >= d, pltpu.roll(flat, d, 2), 0.0)
        total = total + jnp.where(lane < z_cells - d, pltpu.roll(flat, 128 - d, 2), 0.0)
    mean = total * (1.0 / 125.0)
    second = pltpu.roll(mean, 64, 2)
    centre = pltpu.roll(both[2 : 2 + grid_rows], WIDE - 2, 1)
    normed = (centre - mean) * lax.rsqrt(second - mean * mean + epsilon)
    y_at = iota(flat.shape, 0) + (ty * rows - 5)
    x_at = iota(flat.shape, 1)
    x_glob = x_at + (x_first - 5)
    inside = (y_at >= 0) & (y_at < n_ty * rows) & (x_glob >= 0) & (x_glob < 2 * cols)
    inside = inside & (x_at < own + 11) & (iota(flat.shape, 2) < z_cells)
    normed = jnp.where(inside, normed, 0.0).astype(bf16).astype(f32)
    for copy in gathers:
        copy.wait()
    table = jnp.sum(aux[...], axis=0)[:, 0:all_orients]
    eye = iota((all_orients, all_orients), 0) == iota((all_orients, all_orients), 1)
    prior = jnp.sum(jnp.where(eye, table[4:5], 0.0), axis=1, keepdims=True) * prior_step
    high = table[0:4].astype(bf16)
    low = (table[0:4] - high.astype(f32)).astype(bf16)
    factors = jnp.concatenate(
        [high.astype(f32), low.astype(f32), jnp.ones((8, all_orients), f32)], axis=0
    ).astype(bf16)
    blocks = []
    for p in range(pairs):
        block = normed[:, 2 * p : 2 * p + 16, :]
        if 2 * p + 1 < own:
            block = block + pltpu.roll(normed[:, 2 * p + 1 : 2 * p + 17, :], 64, 2)
        blocks.append(block.astype(bf16).reshape(grid_rows * 16, 128))
    stacked = jnp.concatenate(blocks, axis=0)
    for c in range(0, 12, 2):
        moved = jnp.dot(
            stacked, shifts[:, c * 128 : (c + 2) * 128], preferred_element_type=f32
        ).astype(bf16)
        for p in range(pairs):
            part = moved[p * grid_rows * 16 : (p + 1) * grid_rows * 16]
            for e in range(2):
                grid_ref[:, c + e, :, p * 128 : (p + 1) * 128] = part[
                    :, e * 128 : (e + 1) * 128
                ].reshape(grid_rows, 16, 128)

    for leaves, copy in direct:
        pl.when(leaves)(copy.wait_send)
    for mine, arrival, forward in onward:
        pl.when(mine)(forward.wait_send)
        pl.when(jnp.logical_not(mine))(forward.wait_recv)
    cubes = tall[...].reshape(all_orients, 1728)
    for a in range(6):
        tap = jnp.dot(
            cubes[:, a * 288 : (a + 1) * 288], perm, preferred_element_type=f32
        ).astype(bf16)
        for g in range(group):
            weights[g * all_orients : (g + 1) * all_orients, (a + g) * 384 : (a + g + 1) * 384] = tap
    depth = (2 * group + 10) * 192
    for first in range(0, rows, 2 * group):
        for start in (first, first + 1):
            window = grid_ref[start : start + 2 * group + 10].reshape(depth, pairs * 128)
            corr = jnp.dot(weights[...], window, preferred_element_type=f32)
            for g in range(group):
                y = start + 2 * g
                scores = score_scale * corr[g * all_orients : (g + 1) * all_orients] - prior
                peak = jnp.max(scores, axis=0, keepdims=True)
                terms = jnp.exp(scores - peak)
                log_total = peak + jnp.log(jnp.sum(terms, axis=0, keepdims=True))
                firsts = jnp.dot(factors, terms.astype(bf16), preferred_element_type=f32)
                moments = (firsts[0:4] + firsts[4:8]) / firsts[8:9]
                log_ref[y : y + 1, :] = log_total
                for k in range(4):
                    mean_ref[k, y : y + 1, :] = moments[k : k + 1]


def shards(volume, templates, prior_table, moment_table):
    rows, cols, z_cells = volume.shape
    orients = templates.shape[0]
    n_ori = lax.axis_size("ori")
    n_ty = lax.axis_size("ty")
    own = cols // n_ori
    pairs = (own + 1) // 2
    group = min(2, rows // 2)
    lanes = max(128, n_ori * orients)
    vmem = pl.BlockSpec(memory_space=pltpu.VMEM)
    dma = pltpu.SemaphoreType.DMA
    out = pl.pallas_call(
        functools.partial(kernel, n_ori, n_ty, own),
        out_shape=(
            jax.ShapeDtypeStruct((rows, pairs * 128), f32),
            jax.ShapeDtypeStruct((4, rows, pairs * 128), f32),
        ),
        in_specs=[pl.BlockSpec(memory_space=pltpu.HBM)] * 4,
        out_specs=(vmem, vmem),
        scratch_shapes=[
            pltpu.VMEM((3 * rows, 2 * cols + 3 * EDGE, z_cells), f32),
            pltpu.VMEM((n_ori, orients, 1728), bf16),
            pltpu.VMEM((n_ori, 8, lanes), f32),
            pltpu.VMEM((128, 12 * 128), bf16),
            pltpu.VMEM((rows + 11, 12, 16, pairs * 128), bf16),
            pltpu.VMEM((group * n_ori * orients, (2 * group + 10) * 192), bf16),
            pltpu.VMEM((1, orients), jnp.int32),
            pltpu.VMEM((4, orients), f32),
            dma((4,)),
            dma((5,)), dma((5,)),
            dma((n_ori - 1,)), dma((n_ori - 1,)),
            dma((n_ori - 1,)), dma((n_ori - 1,)),
            dma((n_ori - 1,)), dma((n_ori - 1,)),
        ],
        compiler_params=pltpu.CompilerParams(
            collective_id=0, has_side_effects=True, vmem_limit_bytes=55160 * 1024
        ),
    )(volume, templates, prior_table.reshape(1, orients), moment_table)
    return (
        out[0][:, : own * z_cells].reshape(rows, own, z_cells),
        out[1][:, :, : own * z_cells].reshape(4, rows, own, z_cells),
    )


def solution(mesh):
    in_specs = (P(("grp", "ty"), "tx", None), P(("grp", "ori"), None), P("ori"), P(None, "ori"))
    out_specs = (P(("grp", "ty"), ("tx", "ori"), None), P(None, ("grp", "ty"), ("tx", "ori"), None))
    return jax.shard_map(shards, mesh=mesh, in_specs=in_specs, out_specs=out_specs, check_vma=False)
```
